32 devices in a mesh: group: 2 (over x), seq: 2 (over y), mp: 8 (over z, core).
Axes of the slice: x: 2, y: 2, z: 4, core: 2. Of those that a mesh axis runs over, the one named last changes fastest.
Arguments:
- image_tokens: bfloat16 [256, 1280], P(('group', 'seq')), may hold values from -6 to 6
- ln_gain: float32 [1280], replicated, may hold values from 0.25 to 1.75
- ln_bias: float32 [1280], replicated, may hold values from -3 to 3
- mlp_in: bfloat16 [1280, 5120], P(None, 'mp'), may hold values from -0.15625 to 0.15625
- mlp_out: bfloat16 [5120, 1280], P('mp'), may hold values from -0.078125 to 0.078125
- key_proj: bfloat16 [1280, 1024], P(None, 'mp'), may hold values from -0.15625 to 0.15625
- value_proj: bfloat16 [1280, 1024], P(None, 'mp'), may hold values from -0.15625 to 0.15625
- text_tokens: bfloat16 [512, 4096], P(('group', 'seq')), may hold values from -6 to 6
- text_gain: float32 [4096], replicated, may hold values from 0.25 to 1.75
- query_proj: bfloat16 [4096, 4096], P('seq', 'mp'), may hold values from -0.09375 to 0.09375
- output_proj: bfloat16 [4096, 4096], P('seq', 'mp'), may hold values from -0.09375 to 0.09375
- attn_gate: float32 [1], replicated, may hold values from 0.4 to 1.2
- doc_image: int32 [4], P(('group', 'seq')), may hold values from -1 to 1
- out_cotangent: bfloat16 [512, 4096], P(('group', 'seq')), may hold values from -6 to 6
Outputs:
- text_out: bfloat16 [512, 4096], P(('group', 'seq'), 'mp')
- image_grad: float32 [256, 1280], P(('group', 'seq'))
The draws below stay inside these ranges and needn't reach their ends.
Inputs may be any that keep to these rules, and one draw needn't show every extreme that they name: `doc_image`: entry b names the image that text tokens b * 128 to (b + 1) * 128 - 1 read; -1 means the block reads no image.
All inputs are finite; a program needn't handle non-finite values.
Results may differ from the reference program's by a relative error of at most 0.014.
Values may be sent and summed in bfloat16 or wider, within the bound.
A program may use at most 64 MiB of HBM per device.

```python
import jax
import jax.numpy as jnp
from jax import lax

DV = 1280
FFV = 5120
DT = 4096
HT = 128
TQH = 32
KVH = 8
BLOCK = 128
IMG_DEV = 64
IMAGE_ROWS = 256
TEXT = 512
N_GROUP = 2
N_SEQ = 2


def place_ends(result, stream_key, low, largest):
    longest = result.shape.index(max(result.shape))
    spots = []
    for shift in (0, 1):
        where = [jax.random.randint(jax.random.fold_in(stream_key, axis), (), 0, length) for axis, length in enumerate(result.shape)]
        where[longest] = (where[longest] + shift) % result.shape[longest]
        spots.append(tuple(where))
    return result.at[spots[0]].set(low).at[spots[1]].set(largest)


def block_levels(rng, dims, shards, low, top_value):
    gain, own = 1.0, jax.random.fold_in(rng, 6)
    for dim, parts in shards:
        draws = jnp.exp(jax.random.uniform(jax.random.fold_in(own, dim), (parts,), jnp.float32, low / len(shards), top_value / len(shards)))
        gain = gain * jnp.repeat(draws, dims[dim] // parts).reshape([-1 if axis == dim else 1 for axis in range(len(dims))])
    return gain


def normal_values(rng, shape, deviation, bound, cuts=(), dtype=jnp.bfloat16):
    values = deviation * jax.random.normal(rng, shape, jnp.float32)
    if cuts:
        values = values * block_levels(rng, shape, cuts, -0.22, 0.18)
    return jnp.clip(values, -bound, bound).astype(dtype)


def setup_inputs(seed: int = 0) -> dict:
    arg_keys = jax.random.split(jax.random.key(seed), 15)
    image_tokens = normal_values(arg_keys[0], (IMAGE_ROWS, DV), 1.0, 6.0, ((0, 4),))
    ln_gain = jnp.clip(1.0 + 0.15 * jax.random.normal(arg_keys[1], (DV,), jnp.float32), 0.25, 1.75)
    ln_bias = normal_values(arg_keys[2], (DV,), 0.5, 3.0, (), jnp.float32)
    mlp_in = normal_values(arg_keys[3], (DV, FFV), DV ** -0.5, 0.15625, ((1, 8),))
    mlp_out = normal_values(arg_keys[4], (FFV, DV), FFV ** -0.5, 0.078125, ((0, 8),))
    key_proj = normal_values(arg_keys[5], (DV, KVH * HT), DV ** -0.5, 0.15625, ((1, 8),))
    value_proj = normal_values(arg_keys[6], (DV, KVH * HT), DV ** -0.5, 0.15625, ((1, 8),))
    text_tokens = normal_values(arg_keys[7], (TEXT, DT), 1.0, 6.0, ((0, 4),))
    text_gain = jnp.clip(1.0 + 0.15 * jax.random.normal(arg_keys[8], (DT,), jnp.float32), 0.25, 1.75)
    query_proj = normal_values(arg_keys[9], (DT, TQH * HT), DT ** -0.5, 0.09375, ((0, 2), (1, 8)))
    output_proj = normal_values(arg_keys[10], (DT, TQH * HT), (TQH * HT) ** -0.5, 0.09375, ((0, 2), (1, 8)))
    attn_gate = jnp.clip(jax.random.uniform(arg_keys[11], (1,), jnp.float32, 0.4, 1.2), 0.4, 1.2)
    doc_image = place_ends(jax.random.randint(arg_keys[12], (TEXT // BLOCK,), -1, N_GROUP), jax.random.fold_in(arg_keys[12], 1), -1, N_GROUP - 1).astype(jnp.int32)
    out_cotangent = normal_values(arg_keys[13], (TEXT, DT), 1.0, 6.0, ((0, 4),))
    return {"image_tokens": image_tokens, "ln_gain": ln_gain, "ln_bias": ln_bias, "mlp_in": mlp_in, "mlp_out": mlp_out, "key_proj": key_proj, "value_proj": value_proj, "text_tokens": text_tokens, "text_gain": text_gain, "query_proj": query_proj, "output_proj": output_proj, "attn_gate": attn_gate, "doc_image": doc_image, "out_cotangent": out_cotangent}


EPS_VISION = 1e-06
EPS_TEXT = 1e-05
GELU_COEF = 0.7978845608028654
CUBIC_COEF = 0.044715

def rounded(value):
    return lax.optimization_barrier(value.astype(jnp.bfloat16))

def gelu_parts(pre_act):
    cube_term = pre_act * pre_act * pre_act
    tangent = jnp.tanh(GELU_COEF * (pre_act + CUBIC_COEF * cube_term))
    gelu_value = 0.5 * pre_act * (1.0 + tangent)
    gelu_slope = 0.5 * (1.0 + tangent) + 0.5 * pre_act * (1.0 - tangent * tangent) * GELU_COEF * (1.0 + 3.0 * CUBIC_COEF * pre_act * pre_act)
    return (gelu_value, gelu_slope)

def layer_norm(image_tokens, ln_gain, ln_bias):
    image_float = image_tokens.astype(jnp.float32)
    centred = image_float - lax.optimization_barrier(jnp.mean(image_float, axis=1, keepdims=True))
    inv_scale = lax.rsqrt(lax.optimization_barrier(jnp.mean(centred * centred, axis=1, keepdims=True)) + EPS_VISION)
    normed_hat = centred * inv_scale
    normed = (normed_hat * ln_gain + ln_bias).astype(jnp.bfloat16)
    return (image_float, normed_hat, inv_scale, normed)

def norm_backward(d_normed, normed_hat, inv_scale, ln_gain):
    scaled = d_normed * ln_gain
    first_mean = lax.optimization_barrier(jnp.mean(scaled, axis=1, keepdims=True))
    second_mean = lax.optimization_barrier(jnp.mean(scaled * normed_hat, axis=1, keepdims=True))
    return inv_scale * (scaled - first_mean - normed_hat * second_mean)

def contract_last(left, right):
    return lax.dot_general(left, right, (((1,), (1,)), ((), ())), preferred_element_type=jnp.float32)

def reference(image_tokens, ln_gain, ln_bias, mlp_in, mlp_out, key_proj, value_proj, text_tokens, text_gain, query_proj, output_proj, attn_gate, doc_image, out_cotangent):
    highest = lax.Precision.HIGHEST
    image_float, normed_hat, inv_scale, normed = layer_norm(image_tokens, ln_gain, ln_bias)
    pre_act = jnp.dot(normed, mlp_in, preferred_element_type=jnp.float32)
    gelu_value, gelu_slope = gelu_parts(pre_act)
    hidden_act = gelu_value.astype(jnp.bfloat16)
    image_state = (image_float + jnp.dot(hidden_act, mlp_out, preferred_element_type=jnp.float32)).astype(jnp.bfloat16)
    image_keys = rounded(jnp.dot(image_state, key_proj, preferred_element_type=jnp.float32)).astype(jnp.float32).reshape(-1, KVH, HT)
    image_values = rounded(jnp.dot(image_state, value_proj, preferred_element_type=jnp.float32)).astype(jnp.float32).reshape(-1, KVH, HT)
    text_float = text_tokens.astype(jnp.float32)
    text_scale = lax.rsqrt(lax.optimization_barrier(jnp.mean(text_float * text_float, axis=1, keepdims=True)) + EPS_TEXT)
    text_normed = (text_float * text_scale * text_gain).astype(jnp.bfloat16)
    queries = rounded(jnp.dot(text_normed, query_proj, preferred_element_type=jnp.float32)).astype(jnp.float32)
    gate_factor = jnp.tanh(attn_gate[0])
    has_image = (jnp.repeat(doc_image, BLOCK) >= 0).astype(jnp.float32)[:, None]
    d_proj = (gate_factor * has_image * out_cotangent.astype(jnp.float32)).astype(jnp.bfloat16)
    d_attended = rounded(jnp.dot(d_proj, output_proj, preferred_element_type=jnp.float32)).astype(jnp.float32)
    image_len = IMG_DEV * N_SEQ
    block_count = doc_image.shape[0]
    group_size = TQH // KVH
    head_scale = HT ** (-0.5)

    def block_step(carry, inputs):
        key_grads, value_grads = carry
        block_query, block_grad, block_doc = inputs
        chosen = (jnp.maximum(block_doc, 0) * image_len).astype(jnp.int32)
        key_rows = lax.dynamic_slice_in_dim(image_keys, chosen, image_len, 0)
        value_rows = lax.dynamic_slice_in_dim(image_values, chosen, image_len, 0)
        query_heads = block_query.reshape(BLOCK, KVH, group_size, HT)
        grad_heads = block_grad.reshape(BLOCK, KVH, group_size, HT)
        scores = jnp.einsum('tkgd,skd->kgts', query_heads, key_rows, precision=highest) * head_scale
        top_score = lax.optimization_barrier(jnp.max(scores, axis=3, keepdims=True))
        expo_term = jnp.exp(scores - top_score)
        soft_probs = expo_term / lax.optimization_barrier(jnp.sum(expo_term, axis=3, keepdims=True))
        probs_half = rounded(soft_probs).astype(jnp.float32)
        attended = rounded(jnp.einsum('kgts,skd->tkgd', probs_half, value_rows, precision=highest))
        delta_term = lax.optimization_barrier(jnp.sum(grad_heads * attended.astype(jnp.float32), axis=3))
        d_probs = jnp.einsum('tkgd,skd->kgts', grad_heads, value_rows, precision=highest)
        d_scores = rounded(soft_probs * (d_probs - jnp.transpose(delta_term, (1, 2, 0))[..., None])).astype(jnp.float32)
        value_part = jnp.einsum('kgts,tkgd->skd', probs_half, grad_heads, precision=highest)
        key_part = jnp.einsum('kgts,tkgd->skd', d_scores, query_heads, precision=highest) * head_scale
        old_keys = lax.dynamic_slice_in_dim(key_grads, chosen, image_len, 0)
        old_values = lax.dynamic_slice_in_dim(value_grads, chosen, image_len, 0)
        key_grads = lax.dynamic_update_slice_in_dim(key_grads, old_keys + key_part, chosen, 0)
        value_grads = lax.dynamic_update_slice_in_dim(value_grads, old_values + value_part, chosen, 0)
        return ((key_grads, value_grads), attended.reshape(BLOCK, TQH * HT))
    initial = (jnp.zeros((N_GROUP * image_len, KVH, HT), jnp.float32), jnp.zeros((N_GROUP * image_len, KVH, HT), jnp.float32))
    scanned = (queries.reshape(block_count, BLOCK, TQH * HT), d_attended.reshape(block_count, BLOCK, TQH * HT), doc_image)
    (key_grads, value_grads), attended_blocks = lax.scan(block_step, initial, scanned)
    attended_all = attended_blocks.reshape(-1, TQH * HT)
    text_term = contract_last(attended_all, output_proj)
    text_out = (text_float + gate_factor * has_image * text_term).astype(jnp.bfloat16)
    key_flat = key_grads.reshape(-1, KVH * HT)
    value_flat = value_grads.reshape(-1, KVH * HT)
    state_grad = jnp.dot(key_flat, key_proj.astype(jnp.float32).T, precision=highest) + jnp.dot(value_flat, value_proj.astype(jnp.float32).T, precision=highest)
    d_hidden = contract_last(state_grad.astype(jnp.bfloat16), mlp_out)
    d_pre = (d_hidden * gelu_slope).astype(jnp.bfloat16)
    d_normed = contract_last(d_pre, mlp_in)
    image_grad = state_grad + norm_backward(d_normed, normed_hat, inv_scale, ln_gain)
    return (text_out, image_grad)
```

```python
import functools

import jax
import jax.numpy as jnp
from jax import lax
from jax.experimental import pallas as pl
from jax.experimental.pallas import tpu as pltpu
from jax.sharding import PartitionSpec as P

HT = 128
BLOCK = 128


EPS_VISION = 1e-06
EPS_TEXT = 1e-05
GELU_COEF = 0.7978845608028654
CUBIC_COEF = 0.044715


def from_partner(x, axis, stride):
    return lax.ppermute(x, axis, [(i, i ^ 1 << stride) for i in range(lax.axis_size(axis))])


def gelu_parts(pre_act):
    cube_term = pre_act * pre_act * pre_act
    tangent = jnp.tanh(GELU_COEF * (pre_act + CUBIC_COEF * cube_term))
    gelu_value = 0.5 * pre_act * (1.0 + tangent)
    gelu_slope = 0.5 * (1.0 + tangent) + 0.5 * pre_act * (1.0 - tangent * tangent) * GELU_COEF * (
        1.0 + 3.0 * CUBIC_COEF * pre_act * pre_act
    )
    return (gelu_value, gelu_slope)


def layer_norm(image_tokens, ln_gain, ln_bias):
    image_float = image_tokens.astype(jnp.float32)
    centred = image_float - jnp.mean(image_float, axis=1, keepdims=True)
    inv_scale = lax.rsqrt(jnp.mean(centred * centred, axis=1, keepdims=True) + EPS_VISION)
    normed_hat = centred * inv_scale
    normed = (normed_hat * ln_gain + ln_bias).astype(jnp.bfloat16)
    return (image_float, normed_hat, inv_scale, normed)


def norm_backward(d_normed, normed_hat, inv_scale, ln_gain):
    scaled = d_normed * ln_gain
    first_mean = jnp.mean(scaled, axis=1, keepdims=True)
    second_mean = jnp.mean(scaled * normed_hat, axis=1, keepdims=True)
    return inv_scale * (scaled - first_mean - normed_hat * second_mean)


def contract_last(left, right):
    return lax.dot_general(
        left, right, (((1,), (1,)), ((), ())), preferred_element_type=jnp.float32
    )


def attend_block(queries, key_rows, value_rows, d_attended):
    head_scale = queries.shape[3] ** (-0.5)
    scores = (
        jnp.einsum("tkgd,skd->kgts", queries, key_rows, preferred_element_type=jnp.float32)
        * head_scale
    )
    top_score = jnp.max(scores, axis=3, keepdims=True)
    expo_term = jnp.exp(scores - top_score)
    soft_probs = expo_term / jnp.sum(expo_term, axis=3, keepdims=True)
    probs_half = soft_probs.astype(jnp.bfloat16)
    attended = jnp.einsum(
        "kgts,skd->tkgd", probs_half, value_rows, preferred_element_type=jnp.float32
    ).astype(jnp.bfloat16)
    delta_term = jnp.sum(d_attended.astype(jnp.float32) * attended.astype(jnp.float32), axis=3)
    d_probs = jnp.einsum(
        "tkgd,skd->kgts", d_attended, value_rows, preferred_element_type=jnp.float32
    )
    d_scores = (soft_probs * (d_probs - jnp.transpose(delta_term, (1, 2, 0))[..., None])).astype(
        jnp.bfloat16
    )
    value_grads = jnp.einsum(
        "kgts,tkgd->skd", probs_half, d_attended, preferred_element_type=jnp.float32
    )
    key_grads = (
        jnp.einsum("kgts,tkgd->skd", d_scores, queries, preferred_element_type=jnp.float32)
        * head_scale
    )
    return (attended, key_grads, value_grads)


def shards(
    image_tokens,
    ln_gain,
    ln_bias,
    mlp_in,
    mlp_out,
    key_proj,
    value_proj,
    text_tokens,
    text_gain,
    query_proj,
    output_proj,
    attn_gate,
    doc_image,
    out_cotangent,
):
    highest = lax.Precision.HIGHEST
    mp_index = lax.axis_index("mp")
    group_count = lax.axis_size("group")
    seq_count = lax.axis_size("seq")
    image_float, normed_hat, inv_scale, normed = layer_norm(image_tokens, ln_gain, ln_bias)
    pre_act = jnp.dot(normed, mlp_in, preferred_element_type=jnp.float32)
    gelu_value, gelu_slope = gelu_parts(pre_act)
    hidden_act = gelu_value.astype(jnp.bfloat16)
    mlp_term = jnp.dot(hidden_act, mlp_out, preferred_element_type=jnp.float32)
    image_state = (image_float + lax.psum(mlp_term, "mp")).astype(jnp.bfloat16)
    if key_proj.shape[1] < HT:
        partner_key, partner_value = from_partner((key_proj, value_proj), "mp", 0)
        is_odd = mp_index % 2 == 1
        key_cols = jnp.where(
            is_odd,
            jnp.concatenate([partner_key, key_proj], axis=1),
            jnp.concatenate([key_proj, partner_key], axis=1),
        )
        value_cols = jnp.where(
            is_odd,
            jnp.concatenate([partner_value, value_proj], axis=1),
            jnp.concatenate([value_proj, partner_value], axis=1),
        )
    else:
        key_cols = key_proj
        value_cols = value_proj
    kv_width = key_cols.shape[1]
    image_rows = image_tokens.shape[0]
    local_keys = jnp.dot(image_state, key_cols, preferred_element_type=jnp.float32).astype(
        jnp.bfloat16
    )
    local_values = jnp.dot(image_state, value_cols, preferred_element_type=jnp.float32).astype(
        jnp.bfloat16
    )
    key_block = local_keys.reshape(1, 1, image_rows, kv_width)
    value_block = local_values.reshape(1, 1, image_rows, kv_width)
    seq_keys, seq_values = (
        lax.all_gather(key_block, "seq", axis=1, tiled=True),
        lax.all_gather(value_block, "seq", axis=1, tiled=True),
    )
    key_grid, value_grid = (
        lax.all_gather(seq_keys, "group", axis=0, tiled=True),
        lax.all_gather(seq_values, "group", axis=0, tiled=True),
    )
    total_keys = group_count * seq_count * image_rows
    image_len = seq_count * image_rows
    kv_here = kv_width // HT
    key_all = key_grid.reshape(total_keys, kv_here, HT)
    value_all = value_grid.reshape(total_keys, kv_here, HT)
    query_full, output_full = (
        lax.all_gather(query_proj, "seq", axis=0, tiled=True),
        lax.all_gather(output_proj, "seq", axis=0, tiled=True),
    )
    text_float = text_tokens.astype(jnp.float32)
    text_scale = lax.rsqrt(jnp.mean(text_float * text_float, axis=1, keepdims=True) + EPS_TEXT)
    text_normed = (text_float * text_scale * text_gain).astype(jnp.bfloat16)
    text_rows = text_tokens.shape[0]
    block_count = text_rows // BLOCK
    heads_here = query_proj.shape[1] // HT
    group_here = heads_here // kv_here
    queries = jnp.dot(text_normed, query_full, preferred_element_type=jnp.float32).astype(
        jnp.bfloat16
    )
    queries = queries.reshape(block_count, BLOCK, kv_here, group_here, HT)
    token_doc = jnp.repeat(doc_image, BLOCK)
    has_image = (token_doc >= 0).astype(jnp.float32)[:, None]
    gate_factor = jnp.tanh(attn_gate[0])
    d_proj = (gate_factor * has_image * out_cotangent.astype(jnp.float32)).astype(jnp.bfloat16)
    d_attended = jnp.dot(d_proj, output_full, preferred_element_type=jnp.float32).astype(
        jnp.bfloat16
    )
    d_attended = d_attended.reshape(block_count, BLOCK, kv_here, group_here, HT)

    def block_step(carry, inputs):
        key_sums, value_sums = carry
        block_query, block_grad, block_doc = inputs
        chosen = jnp.maximum(block_doc, 0) * image_len
        key_rows = lax.dynamic_slice_in_dim(key_all, chosen, image_len, 0)
        value_rows = lax.dynamic_slice_in_dim(value_all, chosen, image_len, 0)
        attended, key_part, value_part = attend_block(block_query, key_rows, value_rows, block_grad)
        old_keys = lax.dynamic_slice_in_dim(key_sums, chosen, image_len, 0)
        old_values = lax.dynamic_slice_in_dim(value_sums, chosen, image_len, 0)
        key_sums = lax.dynamic_update_slice_in_dim(key_sums, old_keys + key_part, chosen, 0)
        value_sums = lax.dynamic_update_slice_in_dim(value_sums, old_values + value_part, chosen, 0)
        return ((key_sums, value_sums), attended.reshape(BLOCK, heads_here * HT))

    initial = (
        jnp.zeros((total_keys, kv_here, HT), jnp.float32),
        jnp.zeros((total_keys, kv_here, HT), jnp.float32),
    )
    (key_grads, value_grads), attended_blocks = lax.scan(
        block_step, initial, (queries, d_attended, doc_image)
    )
    attended_flat = attended_blocks.reshape(text_rows, heads_here * HT)
    text_term = contract_last(attended_flat, output_full)
    text_share = lax.psum_scatter(
        text_term.astype(jnp.bfloat16), "mp", scatter_dimension=1, tiled=True
    ).astype(jnp.float32)
    out_width = text_share.shape[1]
    text_slice = lax.dynamic_slice_in_dim(text_float, mp_index * out_width, out_width, 1)
    text_out = (text_slice + gate_factor * has_image * text_share).astype(jnp.bfloat16)
    key_pieces = key_grads.reshape(group_count, seq_count, image_rows, kv_width)
    value_pieces = value_grads.reshape(group_count, seq_count, image_rows, kv_width)
    seq_key, seq_value = (
        lax.psum_scatter(key_pieces, "seq", scatter_dimension=1, tiled=True),
        lax.psum_scatter(value_pieces, "seq", scatter_dimension=1, tiled=True),
    )
    key_back, value_back = (
        lax.psum_scatter(
            seq_key.astype(jnp.bfloat16), "group", scatter_dimension=0, tiled=True
        ).astype(jnp.float32),
        lax.psum_scatter(
            seq_value.astype(jnp.bfloat16), "group", scatter_dimension=0, tiled=True
        ).astype(jnp.float32),
    )
    key_back = key_back.reshape(image_rows, kv_width)
    value_back = value_back.reshape(image_rows, kv_width)
    state_term = jnp.dot(key_back, key_cols.astype(jnp.float32).T, precision=highest) + jnp.dot(
        value_back, value_cols.astype(jnp.float32).T, precision=highest
    )
    state_grad = lax.psum(state_term, "mp")
    d_hidden = contract_last(state_grad.astype(jnp.bfloat16), mlp_out)
    d_pre = (d_hidden * gelu_slope).astype(jnp.bfloat16)
    normed_term = contract_last(d_pre, mlp_in)
    d_normed = lax.psum(normed_term.astype(jnp.bfloat16), "mp").astype(jnp.float32)
    image_grad = state_grad + norm_backward(d_normed, normed_hat, inv_scale, ln_gain)
    return (text_out, image_grad)


def fused_kernel(
    dims,
    img_h, gain_ref, bias_ref, mi_h, mo_h, kp_h, vp_h, text_h, tgain_ref, wq_h, wo_h,
    gate_ref, doc_ref, cot_h,
    text_out, grad_out,
    img, mi, mo, kp, vp, xt, ct, tok, wq, wo,
    xn, dp, xr, dr, q_acc, d_acc, q_out, d_out, q_in, d_in,
    nh_buf, inv_buf, slope_buf,
    part1, gath1, sum1, part2, gath2, sum2, part3, gath3, sum3,
    kv_all, gs_out, gs_in, att, t_buf, t_rcv, t_out, fin,
    ld, bsend, brecv, ssend, srecv, rs_s, rs_r, ag_s, ag_r, kv_s, kv_r, gs_s, gs_r,
    at_s, at_r, tb_s, tb_r, fn_s, fn_r,
):
    n_group, n_mp = dims
    f32, bf16 = jnp.float32, jnp.bfloat16
    g, s, m = lax.axis_index("group"), lax.axis_index("seq"), lax.axis_index("mp")
    core = lax.rem(m, 2)
    sibling = (g, s, m + 1 - 2 * core)
    partner = (g, 1 - s, m)
    rows, width = img.shape
    quarter, part_cols = part1.shape[1], part1.shape[2]
    col_parts = width // part_cols
    text_rows, half_cols = xn.shape[1], xn.shape[2]
    half_rows = text_rows // 2
    n_slice = n_mp // 2
    out_width = fin.shape[2]
    heads = q_acc.shape[1] // HT
    pending = []

    def local(src, dst, index):
        copy = pltpu.make_async_copy(src, dst, ld.at[index])
        copy.start()
        return copy

    def send(src, dst, send_sem, recv_sem, device):
        copy = pltpu.make_async_remote_copy(
            src_ref=src, dst_ref=dst, send_sem=send_sem, recv_sem=recv_sem,
            device_id=device, device_id_type=pl.DeviceIdType.MESH,
        )
        copy.start()
        pending.append(copy)

    def arrived(dst, send_sem, recv_sem, device):
        pltpu.make_async_remote_copy(
            src_ref=dst, dst_ref=dst, send_sem=send_sem, recv_sem=recv_sem,
            device_id=device, device_id_type=pl.DeviceIdType.MESH,
        ).wait_recv()

    loads = {}
    for h in range(2):
        cols = pl.ds(h * half_cols, half_cols)
        loads["x%d" % h] = local(text_h.at[:, cols], xt.at[h], h)
        loads["c%d" % h] = local(cot_h.at[:, cols], ct.at[h], 2 + h)
    loads["img"] = local(img_h, img, 4)
    loads["mi"] = local(mi_h, mi, 5)
    loads["mo"] = local(mo_h, mo, 6)
    loads["wq"] = local(wq_h, wq, 7)
    loads["wo"] = local(wo_h, wo, 8)
    loads["kp"] = local(kp_h, kp, 9)
    loads["vp"] = local(vp_h, vp, 10)
    my_cols = pl.ds(pl.multiple_of(m * out_width, out_width), out_width)
    loads["tok"] = local(text_h.at[:, my_cols], tok, 11)

    mates = [(g, s, lax.rem(m + k, n_mp)) for k in range(1, n_mp)]
    quads = [
        (lax.rem(g + dg, n_group), lax.rem(s + ds, 2), m)
        for dg in range(n_group)
        for ds in range(2)
        if dg or ds
    ]
    across = [(g, 1 - s, lax.rem(m + k, n_mp)) for k in range(1, n_mp)]
    barrier = pltpu.get_barrier_semaphore()
    greeted = mates + across + quads
    for device in greeted:
        pl.semaphore_signal(
            barrier, inc=1, device_id=device, device_id_type=pl.DeviceIdType.MESH
        )

    doc = doc_ref[0]
    has_image = jnp.where(doc >= 0, 1.0, 0.0).astype(f32)
    gate_row = jnp.tanh(jnp.full((1, half_cols), gate_ref[0], f32)) * has_image

    step = 16
    steps = half_rows // step

    def norm_rows(half):
        def body(i, carry):
            at = pl.ds(pl.multiple_of(half * half_rows + i * step, step), step)
            left, right = xt[0, at].astype(f32), xt[1, at].astype(f32)
            total = jnp.sum(left * left + right * right, axis=1, keepdims=True)
            scale = lax.rsqrt(total / (2 * half_cols) + EPS_TEXT)
            xn[0, at] = (left * scale * tgain_ref[:, :half_cols]).astype(bf16)
            xn[1, at] = (right * scale * tgain_ref[:, half_cols:]).astype(bf16)
            return carry

        lax.fori_loop(0, steps, body, 0)

    def grad_rows(half):
        def body(i, carry):
            at = pl.ds(pl.multiple_of(half * half_rows + i * step, step), step)
            for h in range(2):
                dp[h, at] = (gate_row * ct[h, at].astype(f32)).astype(bf16)
            return carry

        lax.fori_loop(0, steps, body, 0)

    mine = pl.ds(pl.multiple_of(core * half_rows, half_rows), half_rows)
    theirs = pl.ds(pl.multiple_of((1 - core) * half_rows, half_rows), half_rows)
    loads["x0"].wait()
    loads["x1"].wait()
    norm_rows(core)
    pl.semaphore_wait(barrier, len(greeted))
    send(xn.at[1 - s, mine], xr.at[mine], bsend.at[0], brecv.at[0], partner)
    loads["c0"].wait()
    loads["c1"].wait()
    grad_rows(core)
    send(dp.at[1 - s, mine], dr.at[mine], bsend.at[1], brecv.at[1], partner)

    def scatter(source, index, part, gath):
        for k, device in enumerate(mates):
            send(part.at[device[2]], gath.at[m], rs_s.at[index, k], rs_r.at[index, m], device)

    def scattered(index, part, gath):
        total = part[m].astype(f32)
        for k, device in enumerate(mates):
            arrived(gath.at[device[2]], rs_s.at[index, k], rs_r.at[index, device[2]], device)
            total = total + gath[device[2]].astype(f32)
        return total

    def gather(index, sums, piece):
        sums[m] = piece
        for k, device in enumerate(mates):
            send(sums.at[m], sums.at[m], ag_s.at[index, k], ag_r.at[index, m], device)

    def gathered(index, sums):
        for k, device in enumerate(mates):
            arrived(sums.at[device[2]], ag_s.at[index, k], ag_r.at[index, device[2]], device)
        return jnp.concatenate(
            [
                jnp.concatenate([sums[r * col_parts + c] for c in range(col_parts)], axis=1)
                for r in range(rows // quarter)
            ],
            axis=0,
        )

    def fill(part, c, block):
        for r in range(rows // quarter):
            part[r * col_parts + c] = block[r * quarter : (r + 1) * quarter].astype(bf16)

    loads["img"].wait()
    image_float = img[...].astype(f32)
    centred = image_float - jnp.mean(image_float, axis=1, keepdims=True)
    inv_scale = lax.rsqrt(jnp.mean(centred * centred, axis=1, keepdims=True) + EPS_VISION)
    normed_hat = centred * inv_scale
    nh_buf[...] = normed_hat
    inv_buf[...] = inv_scale
    normed = (normed_hat * gain_ref[...] + bias_ref[...]).astype(bf16)
    loads["mi"].wait()
    pre_act = jnp.dot(normed, mi[...], preferred_element_type=f32)
    gelu_value, gelu_slope = gelu_parts(pre_act)
    slope_buf[...] = gelu_slope
    hidden = gelu_value.astype(bf16)
    loads["mo"].wait()
    for c in range(col_parts):
        cols = slice(c * part_cols, (c + 1) * part_cols)
        fill(part1, c, jnp.dot(hidden, mo[:, cols], preferred_element_type=f32))
    scatter(None, 0, part1, gath1)

    norm_rows(1 - core)
    grad_rows(1 - core)
    loads["wq"].wait()
    q_acc[...] = jnp.dot(xn[s], wq[...], preferred_element_type=f32)
    loads["wo"].wait()
    d_acc[...] = jnp.dot(dp[s], wo[...], preferred_element_type=f32)

    arrived(xr.at[mine], bsend.at[0], brecv.at[0], partner)
    send(xr.at[mine], xr.at[mine], ssend.at[0], srecv.at[0], sibling)

    piece = scattered(0, part1, gath1)
    row_at = pl.ds(pl.multiple_of(lax.div(m, col_parts) * quarter, quarter), quarter)
    col_at = pl.ds(pl.multiple_of(lax.rem(m, col_parts) * part_cols, part_cols), part_cols)
    gather(0, sum1, (img[row_at, col_at].astype(f32) + piece).astype(bf16))

    arrived(xr.at[theirs], ssend.at[0], srecv.at[0], sibling)
    q_out[...] = jnp.dot(xr[...], wq[...], preferred_element_type=f32).astype(bf16)
    send(q_out, q_in, bsend.at[2], brecv.at[2], partner)

    arrived(dr.at[mine], bsend.at[1], brecv.at[1], partner)
    send(dr.at[mine], dr.at[mine], ssend.at[1], srecv.at[1], sibling)

    image_state = gathered(0, sum1)
    loads["kp"].wait()
    loads["vp"].wait()
    here = g * 2 + s
    kv_all[here] = jnp.concatenate(
        [
            jnp.dot(image_state, kp[...], preferred_element_type=f32),
            jnp.dot(image_state, vp[...], preferred_element_type=f32),
        ],
        axis=1,
    ).astype(bf16)
    for k, device in enumerate(quads):
        send(kv_all.at[here], kv_all.at[here], kv_s.at[k], kv_r.at[here], device)

    arrived(dr.at[theirs], ssend.at[1], srecv.at[1], sibling)
    d_out[...] = jnp.dot(dr[...], wo[...], preferred_element_type=f32).astype(bf16)
    send(d_out, d_in, bsend.at[3], brecv.at[3], partner)

    def stacked(block):
        return jnp.concatenate([block[:, h * HT : (h + 1) * HT] for h in range(heads)], axis=0)

    def unstacked(block):
        return jnp.concatenate(
            [block[h * text_rows : (h + 1) * text_rows] for h in range(heads)], axis=1
        )

    head_scale = HT ** (-0.5)
    for k, device in enumerate(quads):
        at = device[0] * 2 + device[1]
        arrived(kv_all.at[at], kv_s.at[k], kv_r.at[at], device)
    chosen = jnp.maximum(doc, 0)
    picks = [jnp.where(chosen == i, 1.0, 0.0).astype(f32) for i in range(n_group)]
    kv = sum(
        picks[i]
        * jnp.concatenate([kv_all[2 * i], kv_all[2 * i + 1]], axis=0).astype(f32)
        for i in range(n_group)
    ).astype(bf16)
    keys, values = kv[:, :HT], kv[:, HT:]
    arrived(q_in, bsend.at[2], brecv.at[2], partner)
    queries = stacked((q_acc[...] + q_in[...].astype(f32)).astype(bf16))
    scores = contract_last(queries, keys) * head_scale
    expo = jnp.exp(scores - jnp.max(scores, axis=1, keepdims=True))
    soft_probs = expo / jnp.sum(expo, axis=1, keepdims=True)
    probs_half = soft_probs.astype(bf16)
    attended = jnp.dot(probs_half, values, preferred_element_type=f32).astype(bf16)
    att[0] = unstacked(attended)
    send(att.at[0], att.at[1], at_s.at[0], at_r.at[0], partner)

    arrived(d_in, bsend.at[3], brecv.at[3], partner)
    d_att = stacked((d_acc[...] + d_in[...].astype(f32)).astype(bf16))
    delta = jnp.sum(d_att.astype(f32) * attended.astype(f32), axis=1, keepdims=True)
    d_scores = (soft_probs * (contract_last(d_att, values) - delta)).astype(bf16)
    first = (((0,), (0,)), ((), ()))
    grads = jnp.concatenate(
        [
            lax.dot_general(d_scores, queries, first, preferred_element_type=f32) * head_scale,
            lax.dot_general(probs_half, d_att, first, preferred_element_type=f32),
        ],
        axis=1,
    )
    for i in range(n_group):
        for j in range(2):
            gs_out[2 * i + j] = (picks[i] * grads[j * rows : (j + 1) * rows]).astype(bf16)
    for k, device in enumerate(quads):
        at = device[0] * 2 + device[1]
        send(gs_out.at[at], gs_in.at[here], gs_s.at[k], gs_r.at[here], device)
    back = gs_out[here].astype(f32)
    for k, device in enumerate(quads):
        at = device[0] * 2 + device[1]
        arrived(gs_in.at[at], gs_s.at[k], gs_r.at[at], device)
        back = back + gs_in[at].astype(f32)
    back = back.astype(bf16)

    for c in range(col_parts):
        cols = slice(c * part_cols, (c + 1) * part_cols)
        fill(
            part2,
            c,
            contract_last(back[:, :HT], kp[cols, :]) + contract_last(back[:, HT:], vp[cols, :]),
        )
    scatter(None, 1, part2, gath2)

    arrived(att.at[1], at_s.at[0], at_r.at[0], partner)
    both = jnp.concatenate([att[0], att[1]], axis=0)
    for j in range(n_slice):
        term = contract_last(both, wo[j * out_width : (j + 1) * out_width, :]).astype(bf16)
        for r in range(2):
            for h in range(2):
                low = r * text_rows + h * half_rows
                t_buf[h, j, r] = term[low : low + half_rows]
        send(t_buf.at[1 - core, j], t_rcv.at[j], tb_s.at[j], tb_r.at[j], sibling)

    gather(1, sum2, scattered(1, part2, gath2).astype(bf16))

    at_self = lax.div(m, n_slice) == s
    place = s * n_slice

    for j in range(n_slice):
        arrived(t_rcv.at[j], tb_s.at[j], tb_r.at[j], sibling)
        t_out[j] = (t_buf[core, j].astype(f32) + t_rcv[j].astype(f32)).astype(bf16)
        send(t_out.at[j, 1], fin.at[m], fn_s.at[j, 1], fn_r.at[m], (g, 1 - s, place + j))
        direct = pltpu.make_async_remote_copy(
            src_ref=t_out.at[j, 0], dst_ref=fin.at[m], send_sem=fn_s.at[j, 0],
            recv_sem=fn_r.at[m], device_id=(g, s, place + j),
            device_id_type=pl.DeviceIdType.MESH,
        )

        @pl.when(m != place + j)
        def _():
            direct.start()

        @pl.when(m == place + j)
        def _():
            fin[m] = t_out[j, 0]

    state_grad = gathered(1, sum2)
    d_hidden = contract_last(state_grad, mo[...])
    d_pre = (d_hidden * slope_buf[...]).astype(bf16)
    for c in range(col_parts):
        cols = slice(c * part_cols, (c + 1) * part_cols)
        fill(part3, c, contract_last(d_pre, mi[cols, :]))
    scatter(None, 2, part3, gath3)
    gather(2, sum3, scattered(2, part3, gath3).astype(bf16))

    loads["tok"].wait()
    for src in range(n_mp):

        @pl.when(jnp.logical_not(jnp.logical_and(at_self, m == src)))
        def _():
            arrived(fin.at[src], fn_s.at[0, 0], fn_r.at[src], (g, 1 - s, src))

    gate_out = gate_row[:, :out_width]
    for h in range(2):
        total = fin[h].astype(f32)
        for z in range(1, n_mp // 2):
            total = total + fin[2 * z + h].astype(f32)
        at = slice(h * half_rows, (h + 1) * half_rows)
        text_out[at] = (tok[at].astype(f32) + gate_out * total).astype(bf16)

    d_normed = gathered(2, sum3).astype(f32)
    grad_out[...] = gathered_state(sum2, rows, quarter, col_parts) + norm_backward(
        d_normed, nh_buf[...], inv_buf[...], gain_ref[...]
    )

    for copy in pending:
        copy.wait_send()
    for j in range(n_slice):

        @pl.when(m != place + j)
        def _():
            pltpu.make_async_remote_copy(
                src_ref=t_out.at[j, 0], dst_ref=fin.at[m], send_sem=fn_s.at[j, 0],
                recv_sem=fn_r.at[m], device_id=(g, s, place + j),
                device_id_type=pl.DeviceIdType.MESH,
            ).wait_send()


def gathered_state(sums, rows, quarter, col_parts):
    return jnp.concatenate(
        [
            jnp.concatenate([sums[r * col_parts + c] for c in range(col_parts)], axis=1)
            for r in range(rows // quarter)
        ],
        axis=0,
    ).astype(jnp.float32)


def fused(
    n_group, n_mp,
    image_tokens, ln_gain, ln_bias, mlp_in, mlp_out, key_proj, value_proj,
    text_tokens, text_gain, query_proj, output_proj, attn_gate, doc_image, out_cotangent,
):
    f32, bf16 = jnp.float32, jnp.bfloat16
    rows, width = image_tokens.shape
    hidden = mlp_in.shape[1]
    text_rows, features = text_tokens.shape
    head_cols = query_proj.shape[1]
    half_cols, half_rows = features // 2, text_rows // 2
    out_width, n_slice = features // n_mp, n_mp // 2
    quarter = 16
    part_cols = width // (n_mp // (rows // quarter))
    pieces = pltpu.VMEM((n_mp, quarter, part_cols), bf16)
    quads = 2 * n_group
    dma = pltpu.SemaphoreType.DMA
    hbm, vmem, smem = (
        pl.BlockSpec(memory_space=space) for space in (pl.ANY, pltpu.VMEM, pltpu.SMEM)
    )
    V = pltpu.VMEM
    scratch = [
        V((rows, width), bf16), V(mlp_in.shape, bf16), V(mlp_out.shape, bf16),
        V(key_proj.shape, bf16), V(value_proj.shape, bf16),
        V((2, text_rows, half_cols), bf16), V((2, text_rows, half_cols), bf16),
        V((text_rows, out_width), bf16),
        V(query_proj.shape, bf16), V(output_proj.shape, bf16),
        V((2, text_rows, half_cols), bf16), V((2, text_rows, half_cols), bf16),
        V((text_rows, half_cols), bf16), V((text_rows, half_cols), bf16),
        V((text_rows, head_cols), f32), V((text_rows, head_cols), f32),
        V((text_rows, head_cols), bf16), V((text_rows, head_cols), bf16),
        V((text_rows, head_cols), bf16), V((text_rows, head_cols), bf16),
        V((rows, width), f32), V((rows, 1), f32), V((rows, hidden), f32),
    ] + [pieces] * 9 + [
        V((quads, rows, 2 * HT), bf16), V((quads, rows, 2 * HT), bf16),
        V((quads, rows, 2 * HT), bf16),
        V((2, text_rows, head_cols), bf16),
        V((2, n_slice, 2, half_rows, out_width), bf16),
        V((n_slice, 2, half_rows, out_width), bf16),
        V((n_slice, 2, half_rows, out_width), bf16),
        V((n_mp, half_rows, out_width), bf16),
        dma((12,)), dma((4,)), dma((4,)), dma((2,)), dma((2,)),
        dma((3, n_mp)), dma((3, n_mp)), dma((3, n_mp)), dma((3, n_mp)),
        dma((quads,)), dma((quads,)), dma((quads,)), dma((quads,)),
        dma((1,)), dma((1,)), dma((n_slice,)), dma((n_slice,)),
        dma((n_slice, 2)), dma((n_mp,)),
    ]
    return pl.pallas_call(
        functools.partial(fused_kernel, (n_group, n_mp)),
        out_shape=(
            jax.ShapeDtypeStruct((text_rows, out_width), bf16),
            jax.ShapeDtypeStruct((rows, width), f32),
        ),
        in_specs=[hbm, vmem, vmem, hbm, hbm, hbm, hbm, hbm, vmem, hbm, hbm, smem, smem, hbm],
        out_specs=(vmem, vmem),
        scratch_shapes=scratch,
        compiler_params=pltpu.CompilerParams(
            collective_id=0, has_side_effects=True, vmem_limit_bytes=44 * 1024 * 1024
        ),
    )(
        image_tokens, ln_gain.reshape(1, -1), ln_bias.reshape(1, -1), mlp_in, mlp_out,
        key_proj, value_proj, text_tokens, text_gain.reshape(1, -1), query_proj, output_proj,
        attn_gate, doc_image, out_cotangent,
    )


def fits(mesh, args):
    n_seq, n_mp = mesh.shape["seq"], mesh.shape["mp"]
    image_tokens, key_proj, text_tokens = args[0], args[5], args[7]
    rows, width = image_tokens.shape
    text_rows, features = text_tokens.shape
    if n_seq != 2 or n_mp % 2 or key_proj.shape[1] != HT or text_rows != BLOCK:
        return False
    if rows % 16 or n_mp % (rows // 16) or features % (n_mp * 128):
        return False
    return width % (n_mp // (rows // 16) * 128) == 0


def solution(mesh):
    def body(*args):
        if fits(mesh, args):
            return fused(mesh.shape["group"], mesh.shape["mp"], *args)
        return shards(*args)

    return jax.shard_map(
        body,
        mesh=mesh,
        in_specs=(
            P(("group", "seq"), None),
            P(),
            P(),
            P(None, "mp"),
            P("mp", None),
            P(None, "mp"),
            P(None, "mp"),
            P(("group", "seq"), None),
            P(),
            P("seq", "mp"),
            P("seq", "mp"),
            P(),
            P(("group", "seq")),
            P(("group", "seq"), None),
        ),
        out_specs=(P(("group", "seq"), "mp"), P(("group", "seq"), None)),
        check_vma=False,
    )
```

```python
import functools

import jax
import jax.numpy as jnp
from jax import lax
from jax.experimental import pallas as pl
from jax.experimental.pallas import tpu as pltpu
from jax.sharding import PartitionSpec as P

HT = 128
BLOCK = 128


EPS_VISION = 1e-06
EPS_TEXT = 1e-05
GELU_COEF = 0.7978845608028654
CUBIC_COEF = 0.044715


def from_partner(x, axis, stride):
    return lax.ppermute(x, axis, [(i, i ^ 1 << stride) for i in range(lax.axis_size(axis))])


def gelu_parts(pre_act):
    cube_term = pre_act * pre_act * pre_act
    tangent = jnp.tanh(GELU_COEF * (pre_act + CUBIC_COEF * cube_term))
    gelu_value = 0.5 * pre_act * (1.0 + tangent)
    gelu_slope = 0.5 * (1.0 + tangent) + 0.5 * pre_act * (1.0 - tangent * tangent) * GELU_COEF * (
        1.0 + 3.0 * CUBIC_COEF * pre_act * pre_act
    )
    return (gelu_value, gelu_slope)


def layer_norm(image_tokens, ln_gain, ln_bias):
    image_float = image_tokens.astype(jnp.float32)
    centred = image_float - jnp.mean(image_float, axis=1, keepdims=True)
    inv_scale = lax.rsqrt(jnp.mean(centred * centred, axis=1, keepdims=True) + EPS_VISION)
    normed_hat = centred * inv_scale
    normed = (normed_hat * ln_gain + ln_bias).astype(jnp.bfloat16)
    return (image_float, normed_hat, inv_scale, normed)


def norm_backward(d_normed, normed_hat, inv_scale, ln_gain):
    scaled = d_normed * ln_gain
    first_mean = jnp.mean(scaled, axis=1, keepdims=True)
    second_mean = jnp.mean(scaled * normed_hat, axis=1, keepdims=True)
    return inv_scale * (scaled - first_mean - normed_hat * second_mean)


def contract_last(left, right):
    return lax.dot_general(
        left, right, (((1,), (1,)), ((), ())), preferred_element_type=jnp.float32
    )


def attend_block(queries, key_rows, value_rows, d_attended):
    head_scale = queries.shape[3] ** (-0.5)
    scores = (
        jnp.einsum("tkgd,skd->kgts", queries, key_rows, preferred_element_type=jnp.float32)
        * head_scale
    )
    top_score = jnp.max(scores, axis=3, keepdims=True)
    expo_term = jnp.exp(scores - top_score)
    soft_probs = expo_term / jnp.sum(expo_term, axis=3, keepdims=True)
    probs_half = soft_probs.astype(jnp.bfloat16)
    attended = jnp.einsum(
        "kgts,skd->tkgd", probs_half, value_rows, preferred_element_type=jnp.float32
    ).astype(jnp.bfloat16)
    delta_term = jnp.sum(d_attended.astype(jnp.float32) * attended.astype(jnp.float32), axis=3)
    d_probs = jnp.einsum(
        "tkgd,skd->kgts", d_attended, value_rows, preferred_element_type=jnp.float32
    )
    d_scores = (soft_probs * (d_probs - jnp.transpose(delta_term, (1, 2, 0))[..., None])).astype(
        jnp.bfloat16
    )
    value_grads = jnp.einsum(
        "kgts,tkgd->skd", probs_half, d_attended, preferred_element_type=jnp.float32
    )
    key_grads = (
        jnp.einsum("kgts,tkgd->skd", d_scores, queries, preferred_element_type=jnp.float32)
        * head_scale
    )
    return (attended, key_grads, value_grads)


def shards(
    image_tokens,
    ln_gain,
    ln_bias,
    mlp_in,
    mlp_out,
    key_proj,
    value_proj,
    text_tokens,
    text_gain,
    query_proj,
    output_proj,
    attn_gate,
    doc_image,
    out_cotangent,
):
    highest = lax.Precision.HIGHEST
    mp_index = lax.axis_index("mp")
    group_count = lax.axis_size("group")
    seq_count = lax.axis_size("seq")
    image_float, normed_hat, inv_scale, normed = layer_norm(image_tokens, ln_gain, ln_bias)
    pre_act = jnp.dot(normed, mlp_in, preferred_element_type=jnp.float32)
    gelu_value, gelu_slope = gelu_parts(pre_act)
    hidden_act = gelu_value.astype(jnp.bfloat16)
    mlp_term = jnp.dot(hidden_act, mlp_out, preferred_element_type=jnp.float32)
    image_state = (image_float + lax.psum(mlp_term, "mp")).astype(jnp.bfloat16)
    if key_proj.shape[1] < HT:
        partner_key, partner_value = from_partner((key_proj, value_proj), "mp", 0)
        is_odd = mp_index % 2 == 1
        key_cols = jnp.where(
            is_odd,
            jnp.concatenate([partner_key, key_proj], axis=1),
            jnp.concatenate([key_proj, partner_key], axis=1),
        )
        value_cols = jnp.where(
            is_odd,
            jnp.concatenate([partner_value, value_proj], axis=1),
            jnp.concatenate([value_proj, partner_value], axis=1),
        )
    else:
        key_cols = key_proj
        value_cols = value_proj
    kv_width = key_cols.shape[1]
    image_rows = image_tokens.shape[0]
    local_keys = jnp.dot(image_state, key_cols, preferred_element_type=jnp.float32).astype(
        jnp.bfloat16
    )
    local_values = jnp.dot(image_state, value_cols, preferred_element_type=jnp.float32).astype(
        jnp.bfloat16
    )
    key_block = local_keys.reshape(1, 1, image_rows, kv_width)
    value_block = local_values.reshape(1, 1, image_rows, kv_width)
    seq_keys, seq_values = (
        lax.all_gather(key_block, "seq", axis=1, tiled=True),
        lax.all_gather(value_block, "seq", axis=1, tiled=True),
    )
    key_grid, value_grid = (
        lax.all_gather(seq_keys, "group", axis=0, tiled=True),
        lax.all_gather(seq_values, "group", axis=0, tiled=True),
    )
    total_keys = group_count * seq_count * image_rows
    image_len = seq_count * image_rows
    kv_here = kv_width // HT
    key_all = key_grid.reshape(total_keys, kv_here, HT)
    value_all = value_grid.reshape(total_keys, kv_here, HT)
    query_full, output_full = (
        lax.all_gather(query_proj, "seq", axis=0, tiled=True),
        lax.all_gather(output_proj, "seq", axis=0, tiled=True),
    )
    text_float = text_tokens.astype(jnp.float32)
    text_scale = lax.rsqrt(jnp.mean(text_float * text_float, axis=1, keepdims=True) + EPS_TEXT)
    text_normed = (text_float * text_scale * text_gain).astype(jnp.bfloat16)
    text_rows = text_tokens.shape[0]
    block_count = text_rows // BLOCK
    heads_here = query_proj.shape[1] // HT
    group_here = heads_here // kv_here
    queries = jnp.dot(text_normed, query_full, preferred_element_type=jnp.float32).astype(
        jnp.bfloat16
    )
    queries = queries.reshape(block_count, BLOCK, kv_here, group_here, HT)
    token_doc = jnp.repeat(doc_image, BLOCK)
    has_image = (token_doc >= 0).astype(jnp.float32)[:, None]
    gate_factor = jnp.tanh(attn_gate[0])
    d_proj = (gate_factor * has_image * out_cotangent.astype(jnp.float32)).astype(jnp.bfloat16)
    d_attended = jnp.dot(d_proj, output_full, preferred_element_type=jnp.float32).astype(
        jnp.bfloat16
    )
    d_attended = d_attended.reshape(block_count, BLOCK, kv_here, group_here, HT)

    def block_step(carry, inputs):
        key_sums, value_sums = carry
        block_query, block_grad, block_doc = inputs
        chosen = jnp.maximum(block_doc, 0) * image_len
        key_rows = lax.dynamic_slice_in_dim(key_all, chosen, image_len, 0)
        value_rows = lax.dynamic_slice_in_dim(value_all, chosen, image_len, 0)
        attended, key_part, value_part = attend_block(block_query, key_rows, value_rows, block_grad)
        old_keys = lax.dynamic_slice_in_dim(key_sums, chosen, image_len, 0)
        old_values = lax.dynamic_slice_in_dim(value_sums, chosen, image_len, 0)
        key_sums = lax.dynamic_update_slice_in_dim(key_sums, old_keys + key_part, chosen, 0)
        value_sums = lax.dynamic_update_slice_in_dim(value_sums, old_values + value_part, chosen, 0)
        return ((key_sums, value_sums), attended.reshape(BLOCK, heads_here * HT))

    initial = (
        jnp.zeros((total_keys, kv_here, HT), jnp.float32),
        jnp.zeros((total_keys, kv_here, HT), jnp.float32),
    )
    (key_grads, value_grads), attended_blocks = lax.scan(
        block_step, initial, (queries, d_attended, doc_image)
    )
    attended_flat = attended_blocks.reshape(text_rows, heads_here * HT)
    text_term = contract_last(attended_flat, output_full)
    text_share = lax.psum_scatter(
        text_term.astype(jnp.bfloat16), "mp", scatter_dimension=1, tiled=True
    ).astype(jnp.float32)
    out_width = text_share.shape[1]
    text_slice = lax.dynamic_slice_in_dim(text_float, mp_index * out_width, out_width, 1)
    text_out = (text_slice + gate_factor * has_image * text_share).astype(jnp.bfloat16)
    key_pieces = key_grads.reshape(group_count, seq_count, image_rows, kv_width)
    value_pieces = value_grads.reshape(group_count, seq_count, image_rows, kv_width)
    seq_key, seq_value = (
        lax.psum_scatter(key_pieces, "seq", scatter_dimension=1, tiled=True),
        lax.psum_scatter(value_pieces, "seq", scatter_dimension=1, tiled=True),
    )
    key_back, value_back = (
        lax.psum_scatter(
            seq_key.astype(jnp.bfloat16), "group", scatter_dimension=0, tiled=True
        ).astype(jnp.float32),
        lax.psum_scatter(
            seq_value.astype(jnp.bfloat16), "group", scatter_dimension=0, tiled=True
        ).astype(jnp.float32),
    )
    key_back = key_back.reshape(image_rows, kv_width)
    value_back = value_back.reshape(image_rows, kv_width)
    state_term = jnp.dot(key_back, key_cols.astype(jnp.float32).T, precision=highest) + jnp.dot(
        value_back, value_cols.astype(jnp.float32).T, precision=highest
    )
    state_grad = lax.psum(state_term, "mp")
    d_hidden = contract_last(state_grad.astype(jnp.bfloat16), mlp_out)
    d_pre = (d_hidden * gelu_slope).astype(jnp.bfloat16)
    normed_term = contract_last(d_pre, mlp_in)
    d_normed = lax.psum(normed_term.astype(jnp.bfloat16), "mp").astype(jnp.float32)
    image_grad = state_grad + norm_backward(d_normed, normed_hat, inv_scale, ln_gain)
    return (text_out, image_grad)


def fused_kernel(
    dims,
    img_h, gain_ref, bias_ref, mi_h, mo_h, kp_h, vp_h, text_h, tgain_ref, wq_h, wo_h,
    gate_ref, doc_ref, cot_h,
    text_out, grad_out,
    img, mi, mo, kp, vp, xt, ct, tok, wq, wo,
    xn, dp, xr, dr, q_acc, d_acc, q_out, d_out, q_in, d_in,
    nh_buf, inv_buf, slope_buf,
    acc, sib_out, sib_in, z_out, z_in, gath,
    kv_all, gs_out, gs_in, att, t_buf, t_rcv, t_out, relay, fin,
    ld, bsend, brecv, ssend, srecv, sb_s, sb_r, rs_s, rs_r, ag_s, ag_r, fw_s, fw_r, kv_s, kv_r, gs_s, gs_r,
    at_s, at_r, tb_s, tb_r, rl_s, rl_r, fn_s, fn_r,
):
    n_group, n_mp = dims
    f32, bf16 = jnp.float32, jnp.bfloat16
    g, s, m = lax.axis_index("group"), lax.axis_index("seq"), lax.axis_index("mp")
    core = lax.rem(m, 2)
    sibling = (g, s, m + 1 - 2 * core)
    partner = (g, 1 - s, m)
    rows, width = img.shape
    chips, chip = n_mp // 2, lax.div(m, 2)
    quarter, half_width = rows // chips, width // 2
    text_rows, half_cols = xn.shape[1], xn.shape[2]
    half_rows = text_rows // 2
    n_slice = n_mp // 2
    out_width = fin.shape[2]
    heads = q_acc.shape[1] // HT
    pending = []
    ln_gain, ln_bias = gain_ref[...][None, :], bias_ref[...][None, :]
    text_gain = tgain_ref[...][None, :]

    def local(src, dst, index):
        copy = pltpu.make_async_copy(src, dst, ld.at[index])
        copy.start()
        return copy

    def send(src, dst, send_sem, recv_sem, device):
        copy = pltpu.make_async_remote_copy(
            src_ref=src, dst_ref=dst, send_sem=send_sem, recv_sem=recv_sem,
            device_id=device, device_id_type=pl.DeviceIdType.MESH,
        )
        copy.start()
        pending.append(copy)

    def arrived(dst, send_sem, recv_sem, device):
        pltpu.make_async_remote_copy(
            src_ref=dst, dst_ref=dst, send_sem=send_sem, recv_sem=recv_sem,
            device_id=device, device_id_type=pl.DeviceIdType.MESH,
        ).wait_recv()

    loads = {}
    for h in range(2):
        cols = pl.ds(h * half_cols, half_cols)
        loads["x%d" % h] = local(text_h.at[:, cols], xt.at[h], h)
        loads["c%d" % h] = local(cot_h.at[:, cols], ct.at[h], 2 + h)
    loads["img"] = local(img_h, img, 4)
    loads["mi"] = local(mi_h, mi, 5)
    loads["mo"] = local(mo_h, mo, 6)
    loads["wq"] = local(wq_h, wq, 7)
    loads["wo"] = local(wo_h, wo, 8)
    loads["kp"] = local(kp_h, kp, 9)
    loads["vp"] = local(vp_h, vp, 10)
    my_cols = pl.ds(pl.multiple_of(m * out_width, out_width), out_width)
    loads["tok"] = local(text_h.at[:, my_cols], tok, 11)

    mates = [(g, s, lax.rem(m + k, n_mp)) for k in range(1, n_mp)]
    quads = [
        (lax.rem(g + dg, n_group), lax.rem(s + ds, 2), m)
        for dg in range(n_group)
        for ds in range(2)
        if dg or ds
    ]
    columns = [(g, s, lax.rem(m + 2 * k, n_mp)) for k in range(1, chips)]
    barrier = pltpu.get_barrier_semaphore()
    greeted = mates + quads
    for device in greeted:
        pl.semaphore_signal(
            barrier, inc=1, device_id=device, device_id_type=pl.DeviceIdType.MESH
        )

    doc = doc_ref[0]
    has_image = jnp.where(doc >= 0, 1.0, 0.0).astype(f32)
    gate_row = jnp.tanh(jnp.full((1, half_cols), gate_ref[0], f32)) * has_image

    step = 16
    steps = half_rows // step

    def norm_rows(half):
        def body(i, carry):
            at = pl.ds(pl.multiple_of(half * half_rows + i * step, step), step)
            left, right = xt[0, at].astype(f32), xt[1, at].astype(f32)
            total = jnp.sum(left * left + right * right, axis=1, keepdims=True)
            scale = lax.rsqrt(total / (2 * half_cols) + EPS_TEXT)
            xn[0, at] = (left * scale * text_gain[:, :half_cols]).astype(bf16)
            xn[1, at] = (right * scale * text_gain[:, half_cols:]).astype(bf16)
            return carry

        lax.fori_loop(0, steps, body, 0)

    def grad_rows(half):
        def body(i, carry):
            at = pl.ds(pl.multiple_of(half * half_rows + i * step, step), step)
            for h in range(2):
                dp[h, at] = (gate_row * ct[h, at].astype(f32)).astype(bf16)
            return carry

        lax.fori_loop(0, steps, body, 0)

    mine = pl.ds(pl.multiple_of(core * half_rows, half_rows), half_rows)
    theirs = pl.ds(pl.multiple_of((1 - core) * half_rows, half_rows), half_rows)
    loads["x0"].wait()
    loads["x1"].wait()
    norm_rows(core)
    pl.semaphore_wait(barrier, len(greeted))
    send(xn.at[1 - s, mine], xr.at[mine], bsend.at[0], brecv.at[0], partner)
    loads["c0"].wait()
    loads["c1"].wait()
    grad_rows(core)
    send(dp.at[1 - s, mine], dr.at[mine], bsend.at[1], brecv.at[1], partner)

    my_half = pl.ds(pl.multiple_of(core * half_width, half_width), half_width)
    its_half = pl.ds(pl.multiple_of((1 - core) * half_width, half_width), half_width)

    def rows_of(at):
        return pl.ds(pl.multiple_of(at * quarter, quarter), quarter)

    def reduce_start(i, term):
        sib_out[i] = term(its_half).astype(bf16)
        send(sib_out.at[i], sib_in.at[i], sb_s.at[i], sb_r.at[i], sibling)
        acc[...] = term(my_half)

    def reduce_cross(i):
        arrived(sib_in.at[i], sb_s.at[i], sb_r.at[i], sibling)
        total = acc[...] + sib_in[i].astype(f32)
        acc[...] = total
        z_out[i] = total.astype(bf16)
        for k, device in enumerate(columns):
            there = lax.div(device[2], 2)
            send(
                z_out.at[i, rows_of(there)], z_in.at[i, chip], rs_s.at[i, k],
                rs_r.at[i, chip], device,
            )

    def reduce_end(i):
        total = acc[rows_of(chip)]
        for k, device in enumerate(columns):
            there = lax.div(device[2], 2)
            arrived(z_in.at[i, there], rs_s.at[i, k], rs_r.at[i, there], device)
            total = total + z_in[i, there].astype(f32)
        return total

    def gather_start(i, piece):
        gath[i, core, rows_of(chip)] = piece
        own = gath.at[i, core, rows_of(chip)]
        for k, device in enumerate(columns):
            send(own, own, ag_s.at[i, k], ag_r.at[i, chip], device)
        send(own, own, fw_s.at[i, 0], fw_r.at[i, chip], sibling)

    def gather_end(i):
        for k, device in enumerate(columns):
            there = lax.div(device[2], 2)
            part = gath.at[i, core, rows_of(there)]
            arrived(part, ag_s.at[i, k], ag_r.at[i, there], device)
            send(part, part, fw_s.at[i, k + 1], fw_r.at[i, there], sibling)
        for there in range(chips):
            part = gath.at[i, 1 - core, rows_of(there)]
            arrived(part, fw_s.at[i, 0], fw_r.at[i, there], sibling)
        return jnp.concatenate([gath[i, 0], gath[i, 1]], axis=1)

    loads["img"].wait()
    image_float = img[...].astype(f32)
    centred = image_float - jnp.mean(image_float, axis=1, keepdims=True)
    inv_scale = lax.rsqrt(jnp.mean(centred * centred, axis=1, keepdims=True) + EPS_VISION)
    normed_hat = centred * inv_scale
    nh_buf[...] = normed_hat
    inv_buf[...] = inv_scale
    normed = (normed_hat * ln_gain + ln_bias).astype(bf16)
    loads["mi"].wait()
    pre_act = jnp.dot(normed, mi[...], preferred_element_type=f32)
    gelu_value, gelu_slope = gelu_parts(pre_act)
    slope_buf[...] = gelu_slope
    hidden = gelu_value.astype(bf16)
    loads["mo"].wait()
    reduce_start(0, lambda cols: jnp.dot(hidden, mo[:, cols], preferred_element_type=f32))

    norm_rows(1 - core)
    reduce_cross(0)
    grad_rows(1 - core)
    loads["wq"].wait()
    q_acc[...] = jnp.dot(xn[s], wq[...], preferred_element_type=f32)
    loads["wo"].wait()
    d_acc[...] = jnp.dot(dp[s], wo[...], preferred_element_type=f32)

    arrived(xr.at[mine], bsend.at[0], brecv.at[0], partner)
    send(xr.at[mine], xr.at[mine], ssend.at[0], srecv.at[0], sibling)

    piece = reduce_end(0)
    gather_start(0, (img[rows_of(chip), my_half].astype(f32) + piece).astype(bf16))

    arrived(xr.at[theirs], ssend.at[0], srecv.at[0], sibling)
    q_out[...] = jnp.dot(xr[...], wq[...], preferred_element_type=f32).astype(bf16)
    send(q_out, q_in, bsend.at[2], brecv.at[2], partner)

    arrived(dr.at[mine], bsend.at[1], brecv.at[1], partner)
    send(dr.at[mine], dr.at[mine], ssend.at[1], srecv.at[1], sibling)

    image_state = gather_end(0)
    loads["kp"].wait()
    loads["vp"].wait()
    here = g * 2 + s
    kv_all[here] = jnp.concatenate(
        [
            jnp.dot(image_state, kp[...], preferred_element_type=f32),
            jnp.dot(image_state, vp[...], preferred_element_type=f32),
        ],
        axis=1,
    ).astype(bf16)
    for k, device in enumerate(quads):
        send(kv_all.at[here], kv_all.at[here], kv_s.at[k], kv_r.at[here], device)

    arrived(dr.at[theirs], ssend.at[1], srecv.at[1], sibling)
    d_out[...] = jnp.dot(dr[...], wo[...], preferred_element_type=f32).astype(bf16)
    send(d_out, d_in, bsend.at[3], brecv.at[3], partner)

    def stacked(block):
        return jnp.concatenate([block[:, h * HT : (h + 1) * HT] for h in range(heads)], axis=0)

    def unstacked(block):
        return jnp.concatenate(
            [block[h * text_rows : (h + 1) * text_rows] for h in range(heads)], axis=1
        )

    head_scale = HT ** (-0.5)
    for k, device in enumerate(quads):
        at = device[0] * 2 + device[1]
        arrived(kv_all.at[at], kv_s.at[k], kv_r.at[at], device)
    chosen = jnp.maximum(doc, 0)
    picks = [jnp.where(chosen == i, 1.0, 0.0).astype(f32) for i in range(n_group)]
    kv = sum(
        picks[i]
        * jnp.concatenate([kv_all[2 * i], kv_all[2 * i + 1]], axis=0).astype(f32)
        for i in range(n_group)
    ).astype(bf16)
    keys, values = kv[:, :HT], kv[:, HT:]
    arrived(q_in, bsend.at[2], brecv.at[2], partner)
    queries = stacked((q_acc[...] + q_in[...].astype(f32)).astype(bf16))
    scores = contract_last(queries, keys) * head_scale
    expo = jnp.exp(scores - jnp.max(scores, axis=1, keepdims=True))
    soft_probs = expo / jnp.sum(expo, axis=1, keepdims=True)
    probs_half = soft_probs.astype(bf16)
    attended = jnp.dot(probs_half, values, preferred_element_type=f32).astype(bf16)
    att[0] = unstacked(attended)
    send(att.at[0], att.at[1], at_s.at[0], at_r.at[0], partner)

    arrived(d_in, bsend.at[3], brecv.at[3], partner)
    d_att = stacked((d_acc[...] + d_in[...].astype(f32)).astype(bf16))
    delta = jnp.sum(d_att.astype(f32) * attended.astype(f32), axis=1, keepdims=True)
    d_scores = (soft_probs * (contract_last(d_att, values) - delta)).astype(bf16)
    first = (((0,), (0,)), ((), ()))
    grads = jnp.concatenate(
        [
            lax.dot_general(d_scores, queries, first, preferred_element_type=f32) * head_scale,
            lax.dot_general(probs_half, d_att, first, preferred_element_type=f32),
        ],
        axis=1,
    )
    for i in range(n_group):
        for j in range(2):
            gs_out[2 * i + j] = (picks[i] * grads[j * rows : (j + 1) * rows]).astype(bf16)
    for k, device in enumerate(quads):
        at = device[0] * 2 + device[1]
        send(gs_out.at[at], gs_in.at[here], gs_s.at[k], gs_r.at[here], device)

    def out_terms(r):
        for j in range(n_slice):
            term = contract_last(att[r], wo[j * out_width : (j + 1) * out_width, :]).astype(bf16)
            for h in range(2):
                t_buf[r, j, h] = term[h * half_rows : (h + 1) * half_rows]
            send(
                t_buf.at[r, j, 1 - core], t_rcv.at[r, j], tb_s.at[r, j], tb_r.at[r, j], sibling
            )

    def out_sum(r, j):
        arrived(t_rcv.at[r, j], tb_s.at[r, j], tb_r.at[r, j], sibling)
        t_out[r, j] = (t_buf[r, j, core].astype(f32) + t_rcv[r, j].astype(f32)).astype(bf16)

    def out_copy(src, r, j):
        return pltpu.make_async_remote_copy(
            src_ref=src, dst_ref=fin.at[m], send_sem=fn_s.at[r, j], recv_sem=fn_r.at[m],
            device_id=(g, s, owner(r, j)), device_id_type=pl.DeviceIdType.MESH,
        )

    def owner(r, j):
        return (s if r == 0 else 1 - s) * n_slice + j

    def out_send(src, r, j):
        @pl.when(m != owner(r, j))
        def _():
            out_copy(src, r, j).start()

        @pl.when(m == owner(r, j))
        def _():
            fin[m] = src[...]

    arrived(att.at[1], at_s.at[0], at_r.at[0], partner)
    out_terms(1)

    back = gs_out[here].astype(f32)
    for k, device in enumerate(quads):
        at = device[0] * 2 + device[1]
        arrived(gs_in.at[at], gs_s.at[k], gs_r.at[at], device)
        back = back + gs_in[at].astype(f32)
    back = back.astype(bf16)

    reduce_start(
        1,
        lambda cols: contract_last(back[:, :HT], kp[cols, :])
        + contract_last(back[:, HT:], vp[cols, :]),
    )
    for j in range(n_slice):
        out_sum(1, j)
        send(t_out.at[1, j], relay.at[j], rl_s.at[j], rl_r.at[j], partner)
    reduce_cross(1)
    out_terms(0)
    gather_start(1, reduce_end(1).astype(bf16))

    state_grad = gather_end(1)
    d_hidden = contract_last(state_grad, mo[...])
    d_pre = (d_hidden * slope_buf[...]).astype(bf16)
    reduce_start(2, lambda cols: contract_last(d_pre, mi[cols, :]))
    reduce_cross(2)
    gather_start(2, reduce_end(2).astype(bf16))
    for j in range(n_slice):
        out_sum(0, j)
        out_send(t_out.at[0, j], 0, j)
    for j in range(n_slice):
        arrived(relay.at[j], rl_s.at[j], rl_r.at[j], partner)
        out_send(relay.at[j], 1, j)
    d_normed = gather_end(2).astype(f32)
    state_grad = jnp.concatenate([gath[1, 0], gath[1, 1]], axis=1).astype(f32)
    grad_out[...] = state_grad + norm_backward(d_normed, nh_buf[...], inv_buf[...], ln_gain)

    loads["tok"].wait()
    for k, device in enumerate(mates):
        arrived(fin.at[device[2]], fn_s.at[0, 0], fn_r.at[device[2]], device)
    gate_out = gate_row[:, :out_width]
    for h in range(2):
        total = fin[h].astype(f32)
        for at in range(1, chips):
            total = total + fin[2 * at + h].astype(f32)
        at = slice(h * half_rows, (h + 1) * half_rows)
        text_out[at] = (tok[at].astype(f32) + gate_out * total).astype(bf16)

    for copy in pending:
        copy.wait_send()
    for j in range(n_slice):
        for r, src in enumerate((t_out.at[0, j], relay.at[j])):

            @pl.when(m != owner(r, j))
            def _():
                out_copy(src, r, j).wait_send()


def fused(
    n_group, n_mp,
    image_tokens, ln_gain, ln_bias, mlp_in, mlp_out, key_proj, value_proj,
    text_tokens, text_gain, query_proj, output_proj, attn_gate, doc_image, out_cotangent,
):
    f32, bf16 = jnp.float32, jnp.bfloat16
    rows, width = image_tokens.shape
    hidden = mlp_in.shape[1]
    text_rows, features = text_tokens.shape
    head_cols = query_proj.shape[1]
    half_cols, half_rows = features // 2, text_rows // 2
    out_width, n_slice = features // n_mp, n_mp // 2
    chips, half_width = n_mp // 2, width // 2
    halves = pltpu.VMEM((3, rows, half_width), bf16)
    quads = 2 * n_group
    dma = pltpu.SemaphoreType.DMA
    hbm, vmem, smem = (
        pl.BlockSpec(memory_space=space) for space in (pl.ANY, pltpu.VMEM, pltpu.SMEM)
    )
    V = pltpu.VMEM
    scratch = [
        V((rows, width), bf16), V(mlp_in.shape, bf16), V(mlp_out.shape, bf16),
        V(key_proj.shape, bf16), V(value_proj.shape, bf16),
        V((2, text_rows, half_cols), bf16), V((2, text_rows, half_cols), bf16),
        V((text_rows, out_width), bf16),
        V(query_proj.shape, bf16), V(output_proj.shape, bf16),
        V((2, text_rows, half_cols), bf16), V((2, text_rows, half_cols), bf16),
        V((text_rows, half_cols), bf16), V((text_rows, half_cols), bf16),
        V((text_rows, head_cols), f32), V((text_rows, head_cols), f32),
        V((text_rows, head_cols), bf16), V((text_rows, head_cols), bf16),
        V((text_rows, head_cols), bf16), V((text_rows, head_cols), bf16),
        V((rows, width), f32), V((rows, 1), f32), V((rows, hidden), f32),
        V((rows, half_width), f32), halves, halves, halves,
        V((3, chips, rows // chips, half_width), bf16), V((3, 2, rows, half_width), bf16),
        V((quads, rows, 2 * HT), bf16), V((quads, rows, 2 * HT), bf16),
        V((quads, rows, 2 * HT), bf16),
        V((2, text_rows, head_cols), bf16),
        V((2, n_slice, 2, half_rows, out_width), bf16),
        V((2, n_slice, half_rows, out_width), bf16),
        V((2, n_slice, half_rows, out_width), bf16),
        V((n_slice, half_rows, out_width), bf16),
        V((n_mp, half_rows, out_width), bf16),
        dma((12,)), dma((4,)), dma((4,)), dma((2,)), dma((2,)),
        dma((3,)), dma((3,)), dma((3, chips)), dma((3, chips)), dma((3, chips)), dma((3, chips)),
        dma((3, chips)), dma((3, chips)),
        dma((quads,)), dma((quads,)), dma((quads,)), dma((quads,)),
        dma((1,)), dma((1,)), dma((2, n_slice)), dma((2, n_slice)),
        dma((n_slice,)), dma((n_slice,)), dma((2, n_slice)), dma((n_mp,)),
    ]
    return pl.pallas_call(
        functools.partial(fused_kernel, (n_group, n_mp)),
        out_shape=(
            jax.ShapeDtypeStruct((text_rows, out_width), bf16),
            jax.ShapeDtypeStruct((rows, width), f32),
        ),
        in_specs=[hbm, vmem, vmem, hbm, hbm, hbm, hbm, hbm, vmem, hbm, hbm, smem, smem, hbm],
        out_specs=(vmem, vmem),
        scratch_shapes=scratch,
        compiler_params=pltpu.CompilerParams(
            collective_id=0, has_side_effects=True, vmem_limit_bytes=60 * 1024 * 1024
        ),
    )(
        image_tokens, ln_gain, ln_bias, mlp_in, mlp_out,
        key_proj, value_proj, text_tokens, text_gain, query_proj, output_proj,
        attn_gate, doc_image, out_cotangent,
    )


def fits(mesh, args):
    n_seq, n_mp = mesh.shape["seq"], mesh.shape["mp"]
    image_tokens, key_proj, text_tokens = args[0], args[5], args[7]
    rows, width = image_tokens.shape
    text_rows, features = text_tokens.shape
    if n_seq != 2 or n_mp % 2 or key_proj.shape[1] != HT or text_rows != BLOCK:
        return False
    return rows == 8 * n_mp and features % (n_mp * 128) == 0 and width % 256 == 0


def solution(mesh):
    def body(*args):
        if fits(mesh, args):
            return fused(mesh.shape["group"], mesh.shape["mp"], *args)
        return shards(*args)

    return jax.shard_map(
        body,
        mesh=mesh,
        in_specs=(
            P(("group", "seq"), None),
            P(),
            P(),
            P(None, "mp"),
            P("mp", None),
            P(None, "mp"),
            P(None, "mp"),
            P(("group", "seq"), None),
            P(),
            P("seq", "mp"),
            P("seq", "mp"),
            P(),
            P(("group", "seq")),
            P(("group", "seq"), None),
        ),
        out_specs=(P(("group", "seq"), "mp"), P(("group", "seq"), None)),
        check_vma=False,
    )
```
